256 devices in a mesh: blk: 32 (over z, x_hi, core), col: 8 (over x_lo, y).
Axes of the slice: x: 4 (x_hi: 2, x_lo: 2; x = x_hi * 2 + x_lo), y: 4, z: 8, core: 2. Of those that a mesh axis runs over, the one named last changes fastest.
Arguments:
- corner_blocks: bfloat16 [32, 65, 288, 288], P('blk'), may hold values from -0.046875 to 0.046875
- diag_shift: float32 [32, 2, 288], P('blk'), may hold values from 0.5 to 2
- sketch: bfloat16 [32, 2, 288, 1024], P('blk', None, None, 'col'), may hold values from -6 to 6
- panel_fold: int32 [32], replicated, may hold values from 0 to 31, each once
Outputs:
- first_image: float32 [32, 2, 288, 1024], P('blk', None, None, 'col')
- second_image: float32 [32, 2, 288, 1024], P('blk', None, None, 'col')
- gram: float32 [1024, 1024], P(None, 'col')
The draws below stay inside these ranges and needn't reach their ends.
Inputs may be any that keep to these rules, and one draw needn't show every extreme that they name: panel_fold holds each of 0 to 31 once.
All inputs are finite; a program needn't handle non-finite values.
Results may differ from the reference program's by a relative error of at most 0.0034.
Values may be sent and summed in bfloat16 or wider, within the bound.
No kernel may reach another device: no remote copies, remote signals or barrier semaphores. Data moves between devices by JAX's collectives and lax.ppermute only.
A program may use at most 192 MiB of HBM per device.

```python
import math
import jax
import jax.numpy as jnp
from jax import lax

ORDER = 18432
SKETCH = 1024
PANELS = 64
PANEL = 288
BLOCKS = 65
N_BLK = 32


def shard_levels(rng, extent, split, least, top_value):
    def one(dim, parts):
        draws = jax.random.uniform(jax.random.fold_in(jax.random.fold_in(rng, 6), dim), (parts,), jnp.float32, least / len(split), top_value / len(split))
        return jnp.repeat(jnp.exp(draws), extent[dim] // parts).reshape((-1,) + (1,) * (len(extent) - dim - 1))

    level = one(*split[0])
    for cut in split[1:]:
        level = level * one(*cut)
    return level


def scatter_about(key, shape, spread, limit, split=(), kind=jnp.bfloat16):
    gain = shard_levels(key, shape, split, -0.22, 0.18) if split else 1.0
    entries = jax.random.normal(key, shape, jnp.float32) * spread * gain
    return jnp.minimum(jnp.maximum(entries, -limit), limit).astype(kind)


def setup_inputs(seed: int = 0) -> dict:
    arg_keys = jax.random.split(jax.random.key(seed), 5)
    corner_blocks = scatter_about(arg_keys[0], (N_BLK, BLOCKS, PANEL, PANEL), ORDER ** -0.5, 0.046875, ((0, 32),))
    diag_shift = jnp.clip(jnp.exp(math.log(2.0) - 1.3862944 * jax.random.uniform(arg_keys[1], (N_BLK, 2, PANEL), jnp.float32) ** shard_levels(arg_keys[1], (N_BLK, 2, PANEL), ((0, 32),), -0.2, 0.2)), 0.5, 2.0)
    sketch = scatter_about(arg_keys[2], (N_BLK, 2, PANEL, SKETCH), 1.0, 6.0, ((0, 32), (3, 8)))
    panel_fold = jax.random.permutation(arg_keys[3], N_BLK).astype(jnp.int32)
    return dict(corner_blocks=corner_blocks, diag_shift=diag_shift, sketch=sketch, panel_fold=panel_fold)


def reference(corner_blocks, diag_shift, sketch, panel_fold):
    panels = PANELS
    slot_panels = jnp.stack([panel_fold, panels - 1 - panel_fold], axis=1).reshape(-1).astype(jnp.int32)

    def to_natural(values):
        flat_values = values.reshape((panels,) + values.shape[2:])
        return jnp.zeros((panels,) + values.shape[2:], values.dtype).at[slot_panels].set(flat_values)

    def to_slots(values):
        return values[slot_panels].reshape((N_BLK, 2) + values.shape[1:])

    block_ids = jnp.arange(BLOCKS, dtype=jnp.int32)
    strict_mask = (jnp.arange(PANEL)[:, None] > jnp.arange(PANEL)[None, :]).astype(jnp.float32)
    shift_nat = to_natural(diag_shift)

    def apply_corner(operand):
        def add_device(totals, stacked):
            blocks, anchor = stacked
            row_panel = jnp.where(block_ids <= anchor, anchor, panels - 1 - anchor).astype(jnp.int32)
            col_panel = jnp.where(block_ids <= anchor, block_ids, block_ids - anchor - 1).astype(jnp.int32)
            masked = blocks.astype(jnp.float32) * jnp.where((row_panel == col_panel)[:, None, None], strict_mask, jnp.ones_like(strict_mask))
            forward = jnp.einsum('bij,bjk->bik', masked, operand[col_panel].astype(jnp.float32))
            mirrored = jnp.einsum('bij,bik->bjk', masked, operand[row_panel].astype(jnp.float32))
            totals = totals.at[row_panel].add(forward).at[col_panel].add(mirrored)
            return totals, None

        start = jnp.zeros((panels, PANEL, SKETCH), jnp.float32)
        totals, unused = lax.scan(add_device, start, (corner_blocks, panel_fold))
        return totals + shift_nat[:, :, None] * operand.astype(jnp.float32)

    first_nat = apply_corner(to_natural(sketch))
    second_nat = apply_corner(first_nat.astype(jnp.bfloat16))
    second_flat = second_nat.astype(jnp.bfloat16).reshape(ORDER, SKETCH)
    gram = jnp.dot(second_flat.T, second_flat, preferred_element_type=jnp.float32) / ORDER
    return to_slots(first_nat), to_slots(second_nat), gram
```

```python
import functools

import jax
import jax.numpy as jnp
import numpy as np
from jax import lax
from jax.experimental import pallas as pl
from jax.experimental.pallas import tpu as pltpu
from jax.sharding import Mesh, PartitionSpec as P

ORDER = 18432
PANELS = 64
PANEL = 288
NZ = 8
ALL = ("z", "xh", "core", "xl", "y")
BLK = ("z", "xh", "core")
COL = ("xl", "y")
FLIP = [(0, 1), (1, 0)]
WINDOW = 40
SHARE = 72


def hop(x, k):
    return lax.ppermute(x, "z", [(i, (i + k) % NZ) for i in range(NZ)])


def ring_gather(x):
    half = x.shape[0] // 2 + 4
    up, down = [x], [x]
    for _ in range(3):
        up.append(hop(up[-1], 1))
        down.append(hop(down[-1], -1))
    far = jnp.concatenate([hop(up[-1][:half], 1), hop(down[-1][half:], -1)])
    return up + [far] + down[:0:-1]


def shares():
    out = []
    for c in range(NZ):
        base, odd = SHARE * (c >> 1), c % 2
        out.append((base + 40 * odd, 40 - 8 * odd, base + 32 * odd, 32 + 8 * odd))
    return out


def row_order():
    order = []
    for s0, n0, s1, n1 in shares():
        order += list(range(s0 // 8, (s0 + n0) // 8))
        order += list(range((PANEL + s1) // 8, (PANEL + s1 + n1) // 8))
    return np.array(order)


def split_rows(x):
    x = x.reshape((SHARE, 8) + x.shape[1:])
    x = jnp.take(x, row_order(), axis=0)
    return x.reshape((NZ, SHARE) + x.shape[2:])


def merge_rows(x):
    x = x.reshape((SHARE, 8) + x.shape[2:])
    x = jnp.take(x, np.argsort(row_order()), axis=0)
    return x.reshape((2 * PANEL,) + x.shape[2:])


def window_kernel(fold, place, blocks, out, held, sems):
    anchor = fold[place[2]]

    def copies(n):
        rows = pl.ds(pl.multiple_of(place[0], 16), WINDOW + 8)
        return [
            pltpu.make_async_copy(blocks.at[index, rows, :], held.at[n, k], sems.at[k])
            for k, index in enumerate(block_pair(anchor, fold[n]))
        ]

    def start(n, carry):
        for copy in copies(n):
            copy.start()
        return carry

    def wait(n, carry):
        for copy in copies(n):
            copy.wait()
        return carry

    def pack(m, carry):
        for k in range(4):
            n = 4 * m + k
            rows = jnp.concatenate([held[n, k].astype(jnp.float32) for k in range(2)], axis=1)
            out[n] = jnp.where(place[1] == 1, rows[8:], rows[:WINDOW]).astype(out.dtype)
        return carry

    lax.fori_loop(0, 32, start, 0)
    lax.fori_loop(0, 32, wait, 0)
    lax.fori_loop(0, 8, pack, 0)


def block_windows(blocks, fold, start, pair):
    place = jnp.stack([start & -16, (start >> 3) & 1, pair])
    return pl.pallas_call(
        window_kernel,
        in_specs=[pl.BlockSpec(memory_space=pltpu.SMEM)] * 2 + [pl.BlockSpec(memory_space=pl.ANY)],
        out_specs=pl.BlockSpec(memory_space=pltpu.VMEM),
        out_shape=jax.ShapeDtypeStruct((32, WINDOW, 2 * PANEL), blocks.dtype),
        scratch_shapes=[
            pltpu.VMEM((32, 2, WINDOW + 8, PANEL), blocks.dtype),
            pltpu.SemaphoreType.DMA((2,)),
        ],
        compiler_params=pltpu.CompilerParams(vmem_limit_bytes=56 * 2**20),
        cost_estimate=pl.CostEstimate(flops=0, bytes_accessed=6 * 2**20, transcendentals=0),
    )(fold, place, blocks)


def block_pair(anchor, partner):
    return partner + anchor + 1, jnp.where(anchor < partner, PANELS - partner + anchor, partner)


def product_kernel(by_rows, places, weights, *refs):
    pieces, out = refs[:32], refs[-1]
    x = jnp.concatenate([piece[...] for piece in pieces], axis=0)
    y = lax.dot_general(
        weights[...], x, (((0,), (0,)), ((), ())), preferred_element_type=jnp.float32
    )
    if by_rows:
        for c, (s0, n0, s1, n1) in enumerate(shares()):
            share = jnp.concatenate([y[s0 : s0 + n0], y[PANEL + s1 : PANEL + s1 + n1]])
            out[c] = share.astype(out.dtype)
    else:
        extra = jnp.concatenate([piece[...] for piece in refs[32:-1]], axis=0)
        for c in range(out.shape[0]):
            columns = slice(128 * c, 128 * c + 128)
            out[c, : 2 * PANEL] = y[:, columns].astype(out.dtype)
            out[c, 2 * PANEL :] = extra[:, columns]


def product(weights, places, pieces, extra=(), width=256):
    depth, rows = weights.shape
    by_rows = not extra
    if by_rows:
        shape, block, place = (NZ, SHARE, 1024), (NZ, SHARE, width), lambda i, at: (0, 0, i)
    else:
        height = rows + SHARE * len(extra)
        shape, block = (NZ, height, 128), (width // 128, height, 128)
        place = lambda i, at: (i, 0, 0)

    def slab(entry):
        if entry is None:
            return pl.BlockSpec((SHARE, width), lambda i, at: (0, i))
        return pl.BlockSpec((None, SHARE, width), lambda i, at: (at[entry], 0, i))

    operands = list(pieces) + [(x, None) for x in extra]
    return pl.pallas_call(
        functools.partial(product_kernel, by_rows),
        grid_spec=pltpu.PrefetchScalarGridSpec(
            num_scalar_prefetch=1,
            grid=(1024 // width,),
            in_specs=[pl.BlockSpec((depth, rows), lambda i, at: (0, 0))]
            + [slab(entry) for _, entry in operands],
            out_specs=pl.BlockSpec(block, place),
        ),
        out_shape=jax.ShapeDtypeStruct(shape, jnp.bfloat16),
        compiler_params=pltpu.CompilerParams(vmem_limit_bytes=60 * 2**20),
        cost_estimate=pl.CostEstimate(
            flops=2 * depth * rows * 1024, bytes_accessed=9 * 2**20, transcendentals=0
        ),
    )(places, weights, *[x for x, _ in operands])


def align(odd, k0, k1):
    even = jnp.concatenate([k0, k1[:32]], axis=0)
    late = jnp.concatenate([k0[8:], k1], axis=0)
    return jnp.where(odd == 1, late, even)


def own_kernel(below, odd, first, second, diagonal, out):
    def place(n):
        t1 = first[n].astype(jnp.float32)
        t2 = second[n].astype(jnp.float32)
        under = below[n] == 1
        zero = jnp.zeros_like(t2)
        k00 = jnp.where(n == 0, diagonal[0], jnp.where(under, zero, t2))
        k11 = jnp.where(n == 0, diagonal[1], jnp.where(under, t2, zero))
        k0 = jnp.concatenate([k00, t1], axis=1)
        k1 = jnp.concatenate([zero, k11], axis=1)
        out[n] = align(odd[0], k0, k1).astype(out.dtype)

    def step(m, carry):
        for k in range(4):
            place(4 * m + k)
        return carry

    lax.fori_loop(0, 8, step, 0)


def merge_kernel(order, below, odd, taken, own, out):
    left = lax.broadcasted_iota(jnp.int32, (WINDOW, 2 * PANEL), 1) < PANEL

    def place(n):
        r = taken[order[n]].astype(jnp.float32)
        turned = jnp.concatenate([r[:, PANEL:], r[:, :PANEL]], axis=1)
        under = below[n] == 1
        k0 = jnp.where(left, jnp.where(under, turned, 0.0), 0.0)
        k1 = jnp.where(left, r, jnp.where(under | (n == 0), 0.0, r))
        out[n] = own[n] + align(odd[0], k0, k1).astype(out.dtype)

    def step(m, carry):
        for k in range(8):
            place(8 * m + k)
        return carry

    lax.fori_loop(0, 4, step, 0)


def on_device(kernel, scalars, arrays):
    return pl.pallas_call(
        kernel,
        in_specs=[pl.BlockSpec(memory_space=pltpu.SMEM)] * len(scalars)
        + [pl.BlockSpec(memory_space=pltpu.VMEM)] * len(arrays),
        out_specs=pl.BlockSpec(memory_space=pltpu.VMEM),
        out_shape=jax.ShapeDtypeStruct((32, SHARE, 2 * PANEL), jnp.bfloat16),
        compiler_params=pltpu.CompilerParams(vmem_limit_bytes=56 * 2**20),
        cost_estimate=pl.CostEstimate(flops=0, bytes_accessed=6 * 2**20, transcendentals=0),
    )(*scalars, *arrays)


def local(corner_blocks, diag_shift, sketch, panel_fold):
    z = lax.axis_index("z")
    core = lax.axis_index("core")
    xh = lax.axis_index("xh")
    e = xh * 2 + core
    c = lax.axis_index("xl") * 4 + lax.axis_index("y")
    odd = c & 1
    anchor = panel_fold[z * 4 + e]
    blocks = corner_blocks[0]
    start = SHARE * (c >> 1) + 32 * odd

    def to_shares(x):
        x = split_rows(x)
        x = lax.all_to_all(jnp.concatenate([x, x]), ("xh",) + COL, 0, 0, tiled=True)
        x = jnp.swapaxes(x.reshape(2, NZ, SHARE, 128), 1, 2)
        return x.reshape(2, SHARE, NZ * 128)

    def gather_operand(x):
        far = lax.ppermute(x, "xh", FLIP)
        near, far = ring_gather(x), ring_gather(far)
        out = []
        for pair in zip(near, far):
            for p in pair:
                out += [p, lax.ppermute(p, "core", FLIP)]
        return [(p, None) for p in out]

    pair = to_shares(sketch[0].reshape(2 * PANEL, 128))
    share = lax.dynamic_index_in_dim(pair, xh, 0, keepdims=False)
    sent = block_windows(blocks, panel_fold, start, z * 4 + e)
    gathered = lax.all_gather(pair, "z", axis=0, tiled=True)
    taken = lax.all_to_all(sent, BLK, 0, 0, tiled=True)

    blocks, pair = lax.optimization_barrier((blocks, pair))
    down = lax.dynamic_slice(blocks, (0, 0, start), (PANELS + 1, PANEL, WINDOW))
    down = jnp.swapaxes(down, 1, 2)

    hops, turn = jnp.arange(NZ)[:, None], jnp.arange(4)[None, :]
    places = ((z - hops) % NZ * 2 + (xh ^ jnp.arange(2)[None, :])).reshape(-1)
    order = (((z - hops) % NZ) * 4 + (e ^ turn)).reshape(-1)
    partner = panel_fold[order]
    below = (anchor < partner).astype(jnp.int32)

    row = start + lax.broadcasted_iota(jnp.int32, (WINDOW, PANEL), 0)
    column = lax.broadcasted_iota(jnp.int32, (WINDOW, PANEL), 1)

    def diagonal(index):
        low = lax.dynamic_slice(blocks, (index, start, 0), (1, WINDOW, PANEL))[0]
        high = lax.dynamic_index_in_dim(down, index, 0, keepdims=False)
        zero = jnp.zeros_like(low)
        return jnp.where(row > column, low, jnp.where(row < column, high, zero))

    diagonals = jnp.stack([diagonal(anchor), diagonal(PANELS)]).astype(jnp.float32)
    own = [jnp.take(down, index, axis=0) for index in block_pair(anchor, partner)]
    odd = odd.reshape(1)
    own = on_device(own_kernel, (below, odd), (*own, diagonals))
    gathered, own, order, places = lax.optimization_barrier((gathered, own, order, places))
    swapped = lax.ppermute(gathered, "core", FLIP)
    pieces = [
        (x, 2 * t + part) for t in range(NZ) for part in range(2) for x in (gathered, swapped)
    ]
    weights = on_device(merge_kernel, (order, below, odd), (taken, own))
    weights = weights.reshape(32 * SHARE, 2 * PANEL)

    shift_rows = diag_shift[0].reshape(2 * PANEL, 1)
    shift_share = lax.dynamic_index_in_dim(split_rows(shift_rows), c, 0, keepdims=False)

    parts = lax.all_to_all(product(weights, places, pieces), COL, 0, 0, tiled=True)
    share = jnp.sum(parts.astype(jnp.float32), axis=0) + shift_share * share.astype(jnp.float32)
    rounded = lax.reduce_precision(share, 8, 7)
    high, low = rounded.astype(jnp.bfloat16), (share - rounded).astype(jnp.bfloat16)
    pieces = gather_operand(high)
    parts = lax.all_to_all(product(weights, places, pieces, (high, low)), COL, 0, 0, tiled=True)
    x = merge_rows(parts[:, 2 * PANEL : 2 * PANEL + SHARE]).astype(jnp.float32)
    first = x + merge_rows(parts[:, 2 * PANEL + SHARE :]).astype(jnp.float32)
    second = jnp.sum(parts[:, : 2 * PANEL].astype(jnp.float32), axis=0) + shift_rows * x
    x = second.astype(jnp.bfloat16)

    rows = lax.all_to_all(jnp.broadcast_to(x, (NZ,) + x.shape), COL, 0, 0, tiled=True)
    rows, first, second = lax.optimization_barrier((rows, first, second))
    part = lax.dot_general(rows, x, (((1,), (0,)), ((), ())), preferred_element_type=jnp.float32)
    part = part.reshape(2, 512, 128)
    mine = lax.dynamic_index_in_dim(part, core, 0, keepdims=False)
    theirs = lax.dynamic_index_in_dim(part, 1 - core, 0, keepdims=False)
    mine = mine + lax.ppermute(theirs, "core", FLIP)
    mine = jnp.sum(lax.all_to_all(mine.reshape(NZ, 64, 128), "z", 0, 0, tiled=True), axis=0)
    mine = (mine + lax.ppermute(mine, "xh", FLIP)) / ORDER
    mine = lax.all_to_all(jnp.broadcast_to(mine, (NZ,) + mine.shape), "z", 0, 0, tiled=True)
    mine = mine.reshape(512, 128)
    other = lax.ppermute(mine, "core", FLIP)
    gram = jnp.where(core == 0, jnp.concatenate([mine, other]), jnp.concatenate([other, mine]))
    return first.reshape(1, 2, PANEL, 128), second.reshape(1, 2, PANEL, 128), gram


def solution(mesh):
    fine = Mesh(mesh.devices.reshape(NZ, 2, 2, 2, 4), ALL)
    return jax.shard_map(
        local,
        mesh=fine,
        in_specs=(P(BLK, None, None, None), P(BLK, None, None), P(BLK, None, None, COL), P()),
        out_specs=(P(BLK, None, None, COL), P(BLK, None, None, COL), P(None, COL)),
        check_vma=False,
    )
```

```python
import functools

import jax
import jax.numpy as jnp
import numpy as np
from jax import lax
from jax.experimental import pallas as pl
from jax.experimental.pallas import tpu as pltpu
from jax.sharding import Mesh, PartitionSpec as P

ORDER = 18432
PANELS = 64
PANEL = 288
NZ = 8
ALL = ("z", "xh", "core", "xl", "y")
BLK = ("z", "xh", "core")
COL = ("xl", "y")
FLIP = [(0, 1), (1, 0)]
WINDOW = 40
SHARE = 72


def hop(x, k):
    return lax.ppermute(x, "z", [(i, (i + k) % NZ) for i in range(NZ)])


def ring_gather(x):
    half = x.shape[0] // 2 + 4
    up, down = [x], [x]
    for _ in range(3):
        up.append(hop(up[-1], 1))
        down.append(hop(down[-1], -1))
    far = jnp.concatenate([hop(up[-1][:half], 1), hop(down[-1][half:], -1)])
    return up + [far] + down[:0:-1]


def shares():
    out = []
    for c in range(NZ):
        base, odd = SHARE * (c >> 1), c % 2
        out.append((base + 40 * odd, 40 - 8 * odd, base + 32 * odd, 32 + 8 * odd))
    return out


def row_order():
    order = []
    for s0, n0, s1, n1 in shares():
        order += list(range(s0 // 8, (s0 + n0) // 8))
        order += list(range((PANEL + s1) // 8, (PANEL + s1 + n1) // 8))
    return np.array(order)


def split_rows(x):
    x = x.reshape((SHARE, 8) + x.shape[1:])
    x = jnp.take(x, row_order(), axis=0)
    return x.reshape((NZ, SHARE) + x.shape[2:])


def merge_rows(x):
    x = x.reshape((SHARE, 8) + x.shape[2:])
    x = jnp.take(x, np.argsort(row_order()), axis=0)
    return x.reshape((2 * PANEL,) + x.shape[2:])


def window_kernel(fold, place, blocks, out, held, sems):
    anchor = fold[place[2]]

    def copies(n):
        rows = pl.ds(pl.multiple_of(place[0], 16), WINDOW + 8)
        return [
            pltpu.make_async_copy(blocks.at[index, rows, :], held.at[n, k], sems.at[k])
            for k, index in enumerate(block_pair(anchor, fold[n]))
        ]

    def start(n, carry):
        for copy in copies(n):
            copy.start()
        return carry

    def wait(n, carry):
        for copy in copies(n):
            copy.wait()
        return carry

    def pack(m, carry):
        for k in range(4):
            n = 4 * m + k
            rows = jnp.concatenate([held[n, k].astype(jnp.float32) for k in range(2)], axis=1)
            out[n] = jnp.where(place[1] == 1, rows[8:], rows[:WINDOW]).astype(out.dtype)
        return carry

    lax.fori_loop(0, 32, start, 0)
    lax.fori_loop(0, 32, wait, 0)
    lax.fori_loop(0, 8, pack, 0)


def block_windows(blocks, fold, start, pair):
    place = jnp.stack([start & -16, (start >> 3) & 1, pair])
    return pl.pallas_call(
        window_kernel,
        in_specs=[pl.BlockSpec(memory_space=pltpu.SMEM)] * 2 + [pl.BlockSpec(memory_space=pl.ANY)],
        out_specs=pl.BlockSpec(memory_space=pltpu.VMEM),
        out_shape=jax.ShapeDtypeStruct((32, WINDOW, 2 * PANEL), blocks.dtype),
        scratch_shapes=[
            pltpu.VMEM((32, 2, WINDOW + 8, PANEL), blocks.dtype),
            pltpu.SemaphoreType.DMA((2,)),
        ],
        compiler_params=pltpu.CompilerParams(vmem_limit_bytes=56 * 2**20),
        cost_estimate=pl.CostEstimate(flops=0, bytes_accessed=6 * 2**20, transcendentals=0),
    )(fold, place, blocks)


def block_pair(anchor, partner):
    return partner + anchor + 1, jnp.where(anchor < partner, PANELS - partner + anchor, partner)


def product_kernel(by_rows, places, weights, *refs):
    pieces, out = refs[:32], refs[-1]
    x = jnp.concatenate([piece[...] for piece in pieces], axis=0)
    y = lax.dot_general(
        weights[...], x, (((0,), (0,)), ((), ())), preferred_element_type=jnp.float32
    )
    if by_rows:
        for c, (s0, n0, s1, n1) in enumerate(shares()):
            share = jnp.concatenate([y[s0 : s0 + n0], y[PANEL + s1 : PANEL + s1 + n1]])
            out[c] = share.astype(out.dtype)
    else:
        extra = jnp.concatenate([piece[...] for piece in refs[32:-1]], axis=0)
        for c in range(out.shape[0]):
            columns = slice(128 * c, 128 * c + 128)
            out[c, : 2 * PANEL] = y[:, columns].astype(out.dtype)
            out[c, 2 * PANEL :] = extra[:, columns]


def product(weights, places, pieces, extra=(), width=512):
    depth, rows = weights.shape
    by_rows = not extra
    if by_rows:
        shape, block, place = (NZ, SHARE, 1024), (NZ, SHARE, width), lambda i, at: (0, 0, i)
    else:
        height = rows + SHARE * len(extra)
        shape, block = (NZ, height, 128), (width // 128, height, 128)
        place = lambda i, at: (i, 0, 0)

    def slab(entry):
        if entry is None:
            return pl.BlockSpec((SHARE, width), lambda i, at: (0, i))
        return pl.BlockSpec((None, SHARE, width), lambda i, at: (at[entry], 0, i))

    operands = list(pieces) + [(x, None) for x in extra]
    return pl.pallas_call(
        functools.partial(product_kernel, by_rows),
        grid_spec=pltpu.PrefetchScalarGridSpec(
            num_scalar_prefetch=1,
            grid=(1024 // width,),
            in_specs=[pl.BlockSpec((depth, rows), lambda i, at: (0, 0))]
            + [slab(entry) for _, entry in operands],
            out_specs=pl.BlockSpec(block, place),
        ),
        out_shape=jax.ShapeDtypeStruct(shape, jnp.bfloat16),
        compiler_params=pltpu.CompilerParams(vmem_limit_bytes=60 * 2**20),
        cost_estimate=pl.CostEstimate(
            flops=2 * depth * rows * 1024, bytes_accessed=9 * 2**20, transcendentals=0
        ),
    )(places, weights, *[x for x, _ in operands])


def align(odd, k0, k1):
    even = jnp.concatenate([k0, k1[:32]], axis=0)
    late = jnp.concatenate([k0[8:], k1], axis=0)
    return jnp.where(odd == 1, late, even)


def own_kernel(below, odd, first, second, diagonal, out):
    def place(n):
        t1 = first[n].astype(jnp.float32)
        t2 = second[n].astype(jnp.float32)
        under = below[n] == 1
        zero = jnp.zeros_like(t2)
        k00 = jnp.where(n == 0, diagonal[0], jnp.where(under, zero, t2))
        k11 = jnp.where(n == 0, diagonal[1], jnp.where(under, t2, zero))
        k0 = jnp.concatenate([k00, t1], axis=1)
        k1 = jnp.concatenate([zero, k11], axis=1)
        out[n] = align(odd[0], k0, k1).astype(out.dtype)

    def step(m, carry):
        for k in range(4):
            place(4 * m + k)
        return carry

    lax.fori_loop(0, 8, step, 0)


def merge_kernel(order, below, odd, taken, own, out):
    left = lax.broadcasted_iota(jnp.int32, (WINDOW, 2 * PANEL), 1) < PANEL

    def place(n):
        r = taken[order[n]].astype(jnp.float32)
        turned = jnp.concatenate([r[:, PANEL:], r[:, :PANEL]], axis=1)
        under = below[n] == 1
        k0 = jnp.where(left, jnp.where(under, turned, 0.0), 0.0)
        k1 = jnp.where(left, r, jnp.where(under | (n == 0), 0.0, r))
        out[n] = own[n] + align(odd[0], k0, k1).astype(out.dtype)

    def step(m, carry):
        for k in range(8):
            place(8 * m + k)
        return carry

    lax.fori_loop(0, 4, step, 0)


def on_device(kernel, scalars, arrays):
    return pl.pallas_call(
        kernel,
        in_specs=[pl.BlockSpec(memory_space=pltpu.SMEM)] * len(scalars)
        + [pl.BlockSpec(memory_space=pltpu.VMEM)] * len(arrays),
        out_specs=pl.BlockSpec(memory_space=pltpu.VMEM),
        out_shape=jax.ShapeDtypeStruct((32, SHARE, 2 * PANEL), jnp.bfloat16),
        compiler_params=pltpu.CompilerParams(vmem_limit_bytes=56 * 2**20),
        cost_estimate=pl.CostEstimate(flops=0, bytes_accessed=6 * 2**20, transcendentals=0),
    )(*scalars, *arrays)


def local(corner_blocks, diag_shift, sketch, panel_fold):
    z = lax.axis_index("z")
    core = lax.axis_index("core")
    xh = lax.axis_index("xh")
    e = xh * 2 + core
    c = lax.axis_index("xl") * 4 + lax.axis_index("y")
    odd = c & 1
    anchor = panel_fold[z * 4 + e]
    blocks = corner_blocks[0]
    start = SHARE * (c >> 1) + 32 * odd

    def to_shares(x):
        x = split_rows(x)
        x = lax.all_to_all(jnp.concatenate([x, x]), ("xh",) + COL, 0, 0, tiled=True)
        x = jnp.swapaxes(x.reshape(2, NZ, SHARE, 128), 1, 2)
        return x.reshape(2, SHARE, NZ * 128)

    def gather_operand(x):
        far = lax.ppermute(x, "xh", FLIP)
        near, far = ring_gather(x), ring_gather(far)
        out = []
        for pair in zip(near, far):
            for p in pair:
                out += [p, lax.ppermute(p, "core", FLIP)]
        return [(p, None) for p in out]

    pair = to_shares(sketch[0].reshape(2 * PANEL, 128))
    share = lax.dynamic_index_in_dim(pair, xh, 0, keepdims=False)
    sent = block_windows(blocks, panel_fold, start, z * 4 + e)
    gathered = lax.all_gather(pair, "z", axis=0, tiled=True)
    taken = lax.all_to_all(sent, BLK, 0, 0, tiled=True)

    blocks, pair = lax.optimization_barrier((blocks, pair))
    down = lax.dynamic_slice(blocks, (0, 0, start), (PANELS + 1, PANEL, WINDOW))
    down = jnp.swapaxes(down, 1, 2)

    hops, turn = jnp.arange(NZ)[:, None], jnp.arange(4)[None, :]
    places = ((z - hops) % NZ * 2 + (xh ^ jnp.arange(2)[None, :])).reshape(-1)
    order = (((z - hops) % NZ) * 4 + (e ^ turn)).reshape(-1)
    partner = panel_fold[order]
    below = (anchor < partner).astype(jnp.int32)

    row = start + lax.broadcasted_iota(jnp.int32, (WINDOW, PANEL), 0)
    column = lax.broadcasted_iota(jnp.int32, (WINDOW, PANEL), 1)

    def diagonal(index):
        low = lax.dynamic_slice(blocks, (index, start, 0), (1, WINDOW, PANEL))[0]
        high = lax.dynamic_index_in_dim(down, index, 0, keepdims=False)
        zero = jnp.zeros_like(low)
        return jnp.where(row > column, low, jnp.where(row < column, high, zero))

    diagonals = jnp.stack([diagonal(anchor), diagonal(PANELS)]).astype(jnp.float32)
    own = [jnp.take(down, index, axis=0) for index in block_pair(anchor, partner)]
    odd = odd.reshape(1)
    own = on_device(own_kernel, (below, odd), (*own, diagonals))
    gathered, own, order, places = lax.optimization_barrier((gathered, own, order, places))
    swapped = lax.ppermute(gathered, "core", FLIP)
    pieces = [
        (x, 2 * t + part) for t in range(NZ) for part in range(2) for x in (gathered, swapped)
    ]
    weights = on_device(merge_kernel, (order, below, odd), (taken, own))
    weights = weights.reshape(32 * SHARE, 2 * PANEL)

    shift_rows = diag_shift[0].reshape(2 * PANEL, 1)
    shift_share = lax.dynamic_index_in_dim(split_rows(shift_rows), c, 0, keepdims=False)

    parts = lax.all_to_all(product(weights, places, pieces), COL, 0, 0, tiled=True)
    share = jnp.sum(parts.astype(jnp.float32), axis=0) + shift_share * share.astype(jnp.float32)
    rounded = lax.reduce_precision(share, 8, 7)
    high, low = rounded.astype(jnp.bfloat16), (share - rounded).astype(jnp.bfloat16)
    pieces = gather_operand(high)
    parts = lax.all_to_all(product(weights, places, pieces, (high, low)), COL, 0, 0, tiled=True)
    x = merge_rows(parts[:, 2 * PANEL : 2 * PANEL + SHARE]).astype(jnp.float32)
    first = x + merge_rows(parts[:, 2 * PANEL + SHARE :]).astype(jnp.float32)
    second = jnp.sum(parts[:, : 2 * PANEL].astype(jnp.float32), axis=0) + shift_rows * x
    x = second.astype(jnp.bfloat16)

    rows = lax.all_to_all(jnp.broadcast_to(x, (NZ,) + x.shape), COL, 0, 0, tiled=True)
    rows, first, second = lax.optimization_barrier((rows, first, second))
    part = lax.dot_general(rows, x, (((1,), (0,)), ((), ())), preferred_element_type=jnp.float32)
    part = part.reshape(2, 512, 128)
    mine = lax.dynamic_index_in_dim(part, core, 0, keepdims=False)
    theirs = lax.dynamic_index_in_dim(part, 1 - core, 0, keepdims=False)
    mine = mine + lax.ppermute(theirs, "core", FLIP)
    mine = jnp.sum(lax.all_to_all(mine.reshape(NZ, 64, 128), "z", 0, 0, tiled=True), axis=0)
    mine = (mine + lax.ppermute(mine, "xh", FLIP)) / ORDER
    mine = lax.all_to_all(jnp.broadcast_to(mine, (NZ,) + mine.shape), "z", 0, 0, tiled=True)
    mine = mine.reshape(512, 128)
    other = lax.ppermute(mine, "core", FLIP)
    gram = jnp.where(core == 0, jnp.concatenate([mine, other]), jnp.concatenate([other, mine]))
    return first.reshape(1, 2, PANEL, 128), second.reshape(1, 2, PANEL, 128), gram


def solution(mesh):
    fine = Mesh(mesh.devices.reshape(NZ, 2, 2, 2, 4), ALL)
    return jax.shard_map(
        local,
        mesh=fine,
        in_specs=(P(BLK, None, None, None), P(BLK, None, None), P(BLK, None, None, COL), P()),
        out_specs=(P(BLK, None, None, COL), P(BLK, None, None, COL), P(None, COL)),
        check_vma=False,
    )
```

```python
import functools

import jax
import jax.numpy as jnp
import numpy as np
from jax import lax
from jax.experimental import pallas as pl
from jax.experimental.pallas import tpu as pltpu
from jax.sharding import Mesh, PartitionSpec as P

ORDER = 18432
PANELS = 64
PANEL = 288
NZ = 8
ALL = ("z", "xh", "core", "xl", "y")
BLK = ("z", "xh", "core")
COL = ("xl", "y")
FLIP = [(0, 1), (1, 0)]
WINDOW = 40
SHARE = 72


def hop(x, k):
    return lax.ppermute(x, "z", [(i, (i + k) % NZ) for i in range(NZ)])


def ring_gather(x):
    half = x.shape[0] // 2 + 4
    up, down = [x], [x]
    for _ in range(3):
        up.append(hop(up[-1], 1))
        down.append(hop(down[-1], -1))
    far = jnp.concatenate([hop(up[-1][:half], 1), hop(down[-1][half:], -1)])
    return up + [far] + down[:0:-1]


def shares():
    out = []
    for c in range(NZ):
        base, odd = SHARE * (c >> 1), c % 2
        out.append((base + 40 * odd, 40 - 8 * odd, base + 32 * odd, 32 + 8 * odd))
    return out


def row_order():
    order = []
    for s0, n0, s1, n1 in shares():
        order += list(range(s0 // 8, (s0 + n0) // 8))
        order += list(range((PANEL + s1) // 8, (PANEL + s1 + n1) // 8))
    return np.array(order)


def split_rows(x):
    x = x.reshape((SHARE, 8) + x.shape[1:])
    x = jnp.take(x, row_order(), axis=0)
    return x.reshape((NZ, SHARE) + x.shape[2:])


def window_kernel(fold, place, blocks, out, held, sems):
    anchor = fold[place[2]]

    def copies(n):
        rows = pl.ds(pl.multiple_of(place[0], 16), WINDOW + 8)
        return [
            pltpu.make_async_copy(blocks.at[index, rows, :], held.at[n, k], sems.at[k])
            for k, index in enumerate(block_pair(anchor, fold[n]))
        ]

    def start(n, carry):
        for copy in copies(n):
            copy.start()
        return carry

    def wait(n, carry):
        for copy in copies(n):
            copy.wait()
        return carry

    def pack(m, carry):
        for k in range(4):
            n = 4 * m + k
            rows = jnp.concatenate([held[n, k].astype(jnp.float32) for k in range(2)], axis=1)
            out[n] = jnp.where(place[1] == 1, rows[8:], rows[:WINDOW]).astype(out.dtype)
        return carry

    lax.fori_loop(0, 32, start, 0)
    lax.fori_loop(0, 32, wait, 0)
    lax.fori_loop(0, 8, pack, 0)


def block_windows(blocks, fold, start, pair):
    place = jnp.stack([start & -16, (start >> 3) & 1, pair])
    return pl.pallas_call(
        window_kernel,
        in_specs=[pl.BlockSpec(memory_space=pltpu.SMEM)] * 2 + [pl.BlockSpec(memory_space=pl.ANY)],
        out_specs=pl.BlockSpec(memory_space=pltpu.VMEM),
        out_shape=jax.ShapeDtypeStruct((32, WINDOW, 2 * PANEL), blocks.dtype),
        scratch_shapes=[
            pltpu.VMEM((32, 2, WINDOW + 8, PANEL), blocks.dtype),
            pltpu.SemaphoreType.DMA((2,)),
        ],
        compiler_params=pltpu.CompilerParams(vmem_limit_bytes=56 * 2**20),
        cost_estimate=pl.CostEstimate(flops=0, bytes_accessed=6 * 2**20, transcendentals=0),
    )(fold, place, blocks)


def block_pair(anchor, partner):
    return partner + anchor + 1, jnp.where(anchor < partner, PANELS - partner + anchor, partner)


def product_kernel(by_rows, places, weights, *refs):
    pieces, out = refs[:32], refs[-1]
    x = jnp.concatenate([piece[...] for piece in pieces], axis=0)
    y = lax.dot_general(
        weights[...], x, (((0,), (0,)), ((), ())), preferred_element_type=jnp.float32
    )
    if by_rows:
        for c, (s0, n0, s1, n1) in enumerate(shares()):
            share = jnp.concatenate([y[s0 : s0 + n0], y[PANEL + s1 : PANEL + s1 + n1]])
            out[c] = share.astype(out.dtype)
    else:
        extra = jnp.concatenate([piece[...] for piece in refs[32:-1]], axis=0)
        for c in range(out.shape[0]):
            columns = slice(128 * c, 128 * c + 128)
            out[c, : 2 * PANEL] = y[:, columns].astype(out.dtype)
            out[c, 2 * PANEL :] = extra[:, columns]


def product(weights, places, pieces, extra=(), width=512):
    depth, rows = weights.shape
    by_rows = not extra
    if by_rows:
        shape, block, place = (NZ, SHARE, 1024), (NZ, SHARE, width), lambda i, at: (0, 0, i)
    else:
        height = rows + SHARE * len(extra)
        shape, block = (NZ, height, 128), (width // 128, height, 128)
        place = lambda i, at: (i, 0, 0)

    def slab(entry):
        if entry is None:
            return pl.BlockSpec((SHARE, width), lambda i, at: (0, i))
        return pl.BlockSpec((None, SHARE, width), lambda i, at: (at[entry], 0, i))

    operands = list(pieces) + [(x, None) for x in extra]
    return pl.pallas_call(
        functools.partial(product_kernel, by_rows),
        grid_spec=pltpu.PrefetchScalarGridSpec(
            num_scalar_prefetch=1,
            grid=(1024 // width,),
            in_specs=[pl.BlockSpec((depth, rows), lambda i, at: (0, 0))]
            + [slab(entry) for _, entry in operands],
            out_specs=pl.BlockSpec(block, place),
        ),
        out_shape=jax.ShapeDtypeStruct(shape, jnp.bfloat16),
        compiler_params=pltpu.CompilerParams(vmem_limit_bytes=60 * 2**20),
        cost_estimate=pl.CostEstimate(
            flops=2 * depth * rows * 1024, bytes_accessed=9 * 2**20, transcendentals=0
        ),
    )(places, weights, *[x for x, _ in operands])


def align(odd, k0, k1):
    even = jnp.concatenate([k0, k1[:32]], axis=0)
    late = jnp.concatenate([k0[8:], k1], axis=0)
    return jnp.where(odd == 1, late, even)


def own_kernel(below, odd, first, second, diagonal, out):
    def place(n):
        t1 = first[n].astype(jnp.float32)
        t2 = second[n].astype(jnp.float32)
        under = below[n] == 1
        zero = jnp.zeros_like(t2)
        k00 = jnp.where(n == 0, diagonal[0], jnp.where(under, zero, t2))
        k11 = jnp.where(n == 0, diagonal[1], jnp.where(under, t2, zero))
        k0 = jnp.concatenate([k00, t1], axis=1)
        k1 = jnp.concatenate([zero, k11], axis=1)
        out[n] = align(odd[0], k0, k1).astype(out.dtype)

    def step(m, carry):
        for k in range(4):
            place(4 * m + k)
        return carry

    lax.fori_loop(0, 8, step, 0)


def merge_kernel(order, below, odd, taken, own, out):
    left = lax.broadcasted_iota(jnp.int32, (WINDOW, 2 * PANEL), 1) < PANEL

    def place(n):
        r = taken[order[n]].astype(jnp.float32)
        turned = jnp.concatenate([r[:, PANEL:], r[:, :PANEL]], axis=1)
        under = below[n] == 1
        k0 = jnp.where(left, jnp.where(under, turned, 0.0), 0.0)
        k1 = jnp.where(left, r, jnp.where(under | (n == 0), 0.0, r))
        out[n] = own[n] + align(odd[0], k0, k1).astype(out.dtype)

    def step(m, carry):
        for k in range(8):
            place(8 * m + k)
        return carry

    lax.fori_loop(0, 4, step, 0)


def on_device(kernel, scalars, arrays):
    return pl.pallas_call(
        kernel,
        in_specs=[pl.BlockSpec(memory_space=pltpu.SMEM)] * len(scalars)
        + [pl.BlockSpec(memory_space=pltpu.VMEM)] * len(arrays),
        out_specs=pl.BlockSpec(memory_space=pltpu.VMEM),
        out_shape=jax.ShapeDtypeStruct((32, SHARE, 2 * PANEL), jnp.bfloat16),
        compiler_params=pltpu.CompilerParams(vmem_limit_bytes=56 * 2**20),
        cost_estimate=pl.CostEstimate(flops=0, bytes_accessed=6 * 2**20, transcendentals=0),
    )(*scalars, *arrays)


def finish_kernel(parts, shift_rows, first, second, wide):
    total = parts[0, : 2 * PANEL].astype(jnp.float32)
    for c in range(1, NZ):
        total += parts[c, : 2 * PANEL].astype(jnp.float32)
    tails = [parts[c, 2 * PANEL :].astype(jnp.float32) for c in range(NZ)]

    def natural(offset):
        upper, lower = [], []
        for tail, (_, n0, _, _) in zip(tails, shares()):
            upper.append(tail[offset : offset + n0])
            lower.append(tail[offset + n0 : offset + SHARE])
        return jnp.concatenate(upper + lower)

    high = natural(0)
    first[...] = high + natural(SHARE)
    result = total + shift_rows[...] * high
    second[...] = result
    for c in range(NZ):
        wide[c] = result.astype(wide.dtype)


def finish(parts, shift_rows):
    image = jax.ShapeDtypeStruct((2 * PANEL, 128), jnp.float32)
    return pl.pallas_call(
        finish_kernel,
        in_specs=[pl.BlockSpec(memory_space=pltpu.VMEM)] * 2,
        out_specs=[pl.BlockSpec(memory_space=pltpu.VMEM)] * 3,
        out_shape=[image, image, jax.ShapeDtypeStruct((NZ, 2 * PANEL, 128), jnp.bfloat16)],
        compiler_params=pltpu.CompilerParams(vmem_limit_bytes=48 * 2**20),
    )(parts, shift_rows)


def gram_kernel(rows, x, out):
    for c in range(NZ):
        out[c] = lax.dot_general(
            rows[c], x[...], (((0,), (0,)), ((), ())), preferred_element_type=jnp.float32
        )


def gram_part(rows, x):
    return pl.pallas_call(
        gram_kernel,
        in_specs=[pl.BlockSpec(memory_space=pltpu.VMEM)] * 2,
        out_specs=pl.BlockSpec(memory_space=pltpu.VMEM),
        out_shape=jax.ShapeDtypeStruct((NZ, 128, 128), jnp.float32),
        compiler_params=pltpu.CompilerParams(vmem_limit_bytes=48 * 2**20),
    )(rows, x)


def local(corner_blocks, diag_shift, sketch, panel_fold):
    z = lax.axis_index("z")
    core = lax.axis_index("core")
    xh = lax.axis_index("xh")
    e = xh * 2 + core
    c = lax.axis_index("xl") * 4 + lax.axis_index("y")
    odd = c & 1
    anchor = panel_fold[z * 4 + e]
    blocks = corner_blocks[0]
    start = SHARE * (c >> 1) + 32 * odd

    def to_shares(x):
        x = split_rows(x)
        x = lax.all_to_all(jnp.concatenate([x, x]), ("xh",) + COL, 0, 0, tiled=True)
        x = jnp.swapaxes(x.reshape(2, NZ, SHARE, 128), 1, 2)
        return x.reshape(2, SHARE, NZ * 128)

    def gather_operand(x):
        far = lax.ppermute(x, "xh", FLIP)
        near, far = ring_gather(x), ring_gather(far)
        out = []
        for pair in zip(near, far):
            for p in pair:
                out += [p, lax.ppermute(p, "core", FLIP)]
        return [(p, None) for p in out]

    pair = to_shares(sketch[0].reshape(2 * PANEL, 128))
    share = lax.dynamic_index_in_dim(pair, xh, 0, keepdims=False)
    sent = block_windows(blocks, panel_fold, start, z * 4 + e)
    gathered = lax.all_gather(pair, "z", axis=0, tiled=True)
    taken = lax.all_to_all(sent, BLK, 0, 0, tiled=True)

    blocks, pair = lax.optimization_barrier((blocks, pair))
    down = lax.dynamic_slice(blocks, (0, 0, start), (PANELS + 1, PANEL, WINDOW))
    down = jnp.swapaxes(down, 1, 2)

    hops, turn = jnp.arange(NZ)[:, None], jnp.arange(4)[None, :]
    places = ((z - hops) % NZ * 2 + (xh ^ jnp.arange(2)[None, :])).reshape(-1)
    order = (((z - hops) % NZ) * 4 + (e ^ turn)).reshape(-1)
    partner = panel_fold[order]
    below = (anchor < partner).astype(jnp.int32)

    row = start + lax.broadcasted_iota(jnp.int32, (WINDOW, PANEL), 0)
    column = lax.broadcasted_iota(jnp.int32, (WINDOW, PANEL), 1)

    def diagonal(index):
        low = lax.dynamic_slice(blocks, (index, start, 0), (1, WINDOW, PANEL))[0]
        high = lax.dynamic_index_in_dim(down, index, 0, keepdims=False)
        zero = jnp.zeros_like(low)
        return jnp.where(row > column, low, jnp.where(row < column, high, zero))

    diagonals = jnp.stack([diagonal(anchor), diagonal(PANELS)]).astype(jnp.float32)
    own = [jnp.take(down, index, axis=0) for index in block_pair(anchor, partner)]
    odd = odd.reshape(1)
    own = on_device(own_kernel, (below, odd), (*own, diagonals))
    gathered, own, order, places = lax.optimization_barrier((gathered, own, order, places))
    swapped = lax.ppermute(gathered, "core", FLIP)
    pieces = [
        (x, 2 * t + part) for t in range(NZ) for part in range(2) for x in (gathered, swapped)
    ]
    weights = on_device(merge_kernel, (order, below, odd), (taken, own))
    weights = weights.reshape(32 * SHARE, 2 * PANEL)

    shift_rows = diag_shift[0].reshape(2 * PANEL, 1)
    shift_share = lax.dynamic_index_in_dim(split_rows(shift_rows), c, 0, keepdims=False)

    parts = lax.all_to_all(product(weights, places, pieces), COL, 0, 0, tiled=True)
    share = jnp.sum(parts.astype(jnp.float32), axis=0) + shift_share * share.astype(jnp.float32)
    rounded = lax.reduce_precision(share, 8, 7)
    high, low = rounded.astype(jnp.bfloat16), (share - rounded).astype(jnp.bfloat16)
    pieces = gather_operand(high)
    parts = lax.all_to_all(product(weights, places, pieces, (high, low)), COL, 0, 0, tiled=True)
    first, second, wide = finish(parts, shift_rows)
    rows = lax.all_to_all(wide, COL, 0, 0, tiled=True)
    part = gram_part(rows, wide[0])
    part = part.reshape(2, 512, 128)
    mine = lax.dynamic_index_in_dim(part, core, 0, keepdims=False)
    theirs = lax.dynamic_index_in_dim(part, 1 - core, 0, keepdims=False)
    mine = mine + lax.ppermute(theirs, "core", FLIP)
    mine = jnp.sum(lax.all_to_all(mine.reshape(NZ, 64, 128), "z", 0, 0, tiled=True), axis=0)
    mine = (mine + lax.ppermute(mine, "xh", FLIP)) / ORDER
    mine = lax.all_to_all(jnp.broadcast_to(mine, (NZ,) + mine.shape), "z", 0, 0, tiled=True)
    mine = mine.reshape(512, 128)
    other = lax.ppermute(mine, "core", FLIP)
    gram = jnp.where(core == 0, jnp.concatenate([mine, other]), jnp.concatenate([other, mine]))
    return first.reshape(1, 2, PANEL, 128), second.reshape(1, 2, PANEL, 128), gram


def solution(mesh):
    fine = Mesh(mesh.devices.reshape(NZ, 2, 2, 2, 4), ALL)
    return jax.shard_map(
        local,
        mesh=fine,
        in_specs=(P(BLK, None, None, None), P(BLK, None, None), P(BLK, None, None, COL), P()),
        out_specs=(P(BLK, None, None, COL), P(BLK, None, None, COL), P(None, COL)),
        check_vma=False,
    )
```
